32 devices in a mesh: ctx: 16 (over z, y, x), head: 2 (over core).
Axes of the slice: x: 2, y: 2, z: 4, core: 2. Of those that a mesh axis runs over, the one named last changes fastest.
Arguments:
- lin_q: bfloat16 [8192, 8, 128], P('ctx', 'head'), may hold values from -1.5 to 1.5
- lin_k: bfloat16 [8192, 8, 128], P('ctx', 'head'), may hold values from -1.5 to 1.5
- lin_v: bfloat16 [8192, 8, 128], P('ctx', 'head'), may hold values from -3 to 3
- lin_dout: bfloat16 [8192, 8, 128], P('ctx', 'head'), may hold values from -0.29882812 to 0.29882812
- lin_decay: float32 [8, 8192], P('head', 'ctx'), may hold values from -1 to 0
- att_q: bfloat16 [8192, 8, 128], P('ctx', 'head'), may hold values from -64 to 64
- att_k: bfloat16 [8192, 128], P('ctx'), may hold values from -6 to 6
- att_v: bfloat16 [8192, 128], P('ctx'), may hold values from -6 to 6
- att_dout: bfloat16 [8192, 8, 128], P('ctx', 'head'), may hold values from -1.796875 to 1.796875
- doc_block: int32 [32], replicated, may hold values from 0 to 4, as said below
Outputs:
- lin_dq: bfloat16 [8192, 8, 128], P('ctx', 'head')
- lin_dk: bfloat16 [8192, 8, 128], P('ctx', 'head')
- lin_dv: bfloat16 [8192, 8, 128], P('ctx', 'head')
- att_dq: bfloat16 [8192, 8, 128], P('ctx', 'head')
- att_dk: bfloat16 [8192, 128], P(('ctx', 'head'))
- att_dv: bfloat16 [8192, 128], P(('ctx', 'head'))
The draws below stay inside these ranges and needn't reach their ends.
Inputs may be any that keep to these rules, and one draw needn't show every extreme that they name: doc_block starts at 0, never falls and rises by at most one from block to block; each document spans 1 to 12 blocks; the first spans exactly 12.
All inputs are finite; a program needn't handle non-finite values.
Results may differ from the reference program's by a relative error of at most 0.0052.
Values may be sent and summed in bfloat16 or wider, within the bound.
A program may use at most 128 MiB of HBM per device.

```python
import math
import jax
import jax.numpy as jnp
from jax import lax

HD = 128
TILE_WIDTH = 256
MOST_BLK = 12
TILE_NUMBER = 32
SEQ = 8192
LINEAR_ATTN_COUNT = 8
QHEADS = 8
DOCS = 5


def attention_pair(key):
    starting_number = jax.random.fold_in(key, 17)
    query_key, key_key = jax.random.split(starting_number, 2)
    queries = jnp.clip(jax.random.normal(query_key, (SEQ, QHEADS, HD), jnp.float32), -6.0, 6.0)
    keys_out = jnp.clip(jax.random.normal(key_key, (SEQ, HD), jnp.float32), -6.0, 6.0)
    return (queries, keys_out)


def draw_att_q(key, part):
    return attention_pair(key)[0].astype(jnp.bfloat16)


def draw_att_k(key, part):
    return attention_pair(key)[1].astype(jnp.bfloat16)


def draw_doc_block(key, part):
    starting_number = jax.random.fold_in(key, 41)
    others = DOCS - 1
    remaining = TILE_NUMBER - MOST_BLK
    extra = remaining - others
    capacity = MOST_BLK - 1
    slots = jnp.arange(others * capacity, dtype=jnp.int32) // capacity
    shuffled = jax.random.permutation(starting_number, slots)
    chosen = shuffled[:extra]
    counts = jnp.sum((chosen[:, None] == jnp.arange(others, dtype=jnp.int32)[None, :]).astype(jnp.int32), axis=0)
    ends = jnp.cumsum(1 + counts)
    blocks = jnp.arange(remaining, dtype=jnp.int32)
    later_ids = 1 + jnp.sum((blocks[:, None] >= ends[None, :]).astype(jnp.int32), axis=1)
    return jnp.concatenate([jnp.zeros((MOST_BLK,), jnp.int32), later_ids.astype(jnp.int32)])


def draw_lin_decay(key, part):
    starting_number = jax.random.fold_in(key, 29)
    permute_prng_seed, gradual_prng_seed, quick_prng_seed, tile_prng_seed, position_prng_seed, spurt_prng_seed, objective_prng_seed = jax.random.split(starting_number, 7)
    joined_positions = MOST_BLK * TILE_WIDTH
    fast_count = LINEAR_ATTN_COUNT // 2
    order = jax.random.permutation(permute_prng_seed, LINEAR_ATTN_COUNT)
    fast = order < fast_count
    slow_rate = jax.random.uniform(gradual_prng_seed, (LINEAR_ATTN_COUNT,), jnp.float32, 0.1, 0.5) / joined_positions
    fast_rate = jax.random.uniform(quick_prng_seed, (LINEAR_ATTN_COUNT,), jnp.float32, 1.0 / 50.0, 1.0 / 30.0)
    rate = jnp.where(fast, fast_rate, slow_rate)
    spread = math.log(2.0)
    block_factor = jnp.exp(jax.random.uniform(tile_prng_seed, (LINEAR_ATTN_COUNT, TILE_NUMBER, 1), jnp.float32, -spread, spread))
    token_factor = jnp.exp(jax.random.uniform(position_prng_seed, (LINEAR_ATTN_COUNT, TILE_NUMBER, TILE_WIDTH), jnp.float32, -spread, spread))
    constant_fraction = -rate[:, None, None] * block_factor * token_factor
    spurt_extents = jax.random.bernoulli(spurt_prng_seed, 3.0 / joined_positions, (LINEAR_ATTN_COUNT, TILE_NUMBER, TILE_WIDTH))
    objective_numbers = jax.random.uniform(objective_prng_seed, (LINEAR_ATTN_COUNT, TILE_NUMBER, TILE_WIDTH), jnp.float32, math.log(0.5), math.log(0.8))
    ultimate_outcome = constant_fraction + jnp.where(spurt_extents, objective_numbers, 0.0)
    return jnp.clip(ultimate_outcome, -1.0, 0.0).reshape(LINEAR_ATTN_COUNT, SEQ)


def block_scale(key, extent, cuts, least, high):
    factor_of = 1.0
    for axis_at, shards_of in cuts:
        steps = jax.random.uniform(jax.random.fold_in(jax.random.fold_in(key, 6), axis_at), (shards_of,), jnp.float32, least / len(cuts), high / len(cuts))
        factor_of = factor_of * jnp.repeat(jnp.exp(steps), extent[axis_at] // shards_of).reshape((-1,) + (1,) * (len(extent) - 1 - axis_at))
    return factor_of


def noise(stream_key, extent, scale, limit, cuts=(), kind=jnp.bfloat16):
    level = block_scale(stream_key, extent, cuts, -0.22, 0.18) if cuts else 1.0
    entries = jax.random.normal(stream_key, extent, jnp.float32) * scale * level
    return jnp.minimum(jnp.maximum(entries, -limit), limit).astype(kind)


def setup_inputs(seed: int = 0) -> dict:
    seeds = jax.random.split(jax.random.key(seed), 11)
    return {
        "lin_q": noise(seeds[0], (SEQ, LINEAR_ATTN_COUNT, HD), 0.25, 1.5, ((0, 16), (1, 2))),
        "lin_k": noise(seeds[1], (SEQ, LINEAR_ATTN_COUNT, HD), 0.25, 1.5, ((0, 16), (1, 2))),
        "lin_v": noise(seeds[2], (SEQ, LINEAR_ATTN_COUNT, HD), 0.5, 3.0, ((0, 16), (1, 2))),
        "lin_dout": noise(seeds[3], (SEQ, LINEAR_ATTN_COUNT, HD), 0.05, 0.29882812, ((0, 16), (1, 2))),
        "lin_decay": draw_lin_decay(jax.random.fold_in(seeds[10], 71), 0),
        "att_q": draw_att_q(jax.random.fold_in(seeds[10], 71), 0),
        "att_k": draw_att_k(jax.random.fold_in(seeds[10], 71), 0),
        "att_v": noise(seeds[7], (SEQ, HD), 1.0, 6.0, ((0, 16),)),
        "att_dout": noise(seeds[8], (SEQ, QHEADS, HD), 0.3, 1.796875, ((0, 16), (1, 2))),
        "doc_block": draw_doc_block(jax.random.fold_in(seeds[10], 71), 0),
    }


NEG = -1e30


def rounded(values):
    return lax.optimization_barrier(values.astype(jnp.bfloat16)).astype(jnp.float32)


def block_terms(queries, keys_in, values, douts, decay):
    highest = lax.Precision.HIGHEST
    queries = queries.astype(jnp.float32)
    keys_in = keys_in.astype(jnp.float32)
    values = values.astype(jnp.float32)
    douts = douts.astype(jnp.float32)
    cumulative = jnp.cumsum(decay, axis=1)
    block_total = cumulative[:, -1]
    offsets = jnp.arange(decay.shape[1], dtype=jnp.int32)
    lower_tri = (offsets[:, None] >= offsets[None, :])[None]
    spread = jnp.where(lower_tri, cumulative[:, :, None] - cumulative[:, None, :], 0.0)
    weights = jnp.where(lower_tri, jnp.exp(spread), 0.0)
    cross = jnp.einsum("thd,shd->hts", douts, values)
    inner = jnp.einsum("thd,shd->hts", queries, keys_in)
    left_mix = rounded(cross * weights)
    right_mix = rounded(inner * weights)
    grad_query = jnp.einsum("hts,shd->thd", left_mix, keys_in)
    grad_key = jnp.einsum("hts,thd->shd", left_mix, queries)
    grad_value = jnp.einsum("hts,thd->shd", right_mix, douts)
    head_decay = jnp.exp(cumulative).T[:, :, None]
    tail_decay = jnp.exp(block_total[:, None] - cumulative).T[:, :, None]
    key_state = jnp.einsum("shi,shj->hij", keys_in * tail_decay, values, precision=highest)
    query_state = jnp.einsum("thi,thj->hij", queries * head_decay, douts, precision=highest)
    return grad_query, grad_key, grad_value, head_decay, tail_decay, block_total, key_state, query_state


def finish(terms, keys_in, values, douts, into, back):
    highest = lax.Precision.HIGHEST
    grad_query, grad_key, grad_value, head_decay, tail_decay, block_total, key_state, query_state = terms
    grad_query = grad_query + head_decay * jnp.einsum("thj,hij->thi", douts.astype(jnp.float32), into, precision=highest)
    grad_key = grad_key + tail_decay * jnp.einsum("shj,hij->shi", values.astype(jnp.float32), back, precision=highest)
    grad_value = grad_value + tail_decay * jnp.einsum("shi,hij->shj", keys_in.astype(jnp.float32), back, precision=highest)
    return grad_query.astype(jnp.bfloat16), grad_key.astype(jnp.bfloat16), grad_value.astype(jnp.bfloat16)


def lightning_grads(lin_q, lin_k, lin_v, lin_dout, lin_decay, doc_block):
    block_shape = (TILE_NUMBER, TILE_WIDTH, LINEAR_ATTN_COUNT, HD)
    queries = lin_q.reshape(block_shape)
    keys_in = lin_k.reshape(block_shape)
    values = lin_v.reshape(block_shape)
    douts = lin_dout.reshape(block_shape)
    decay = lin_decay.reshape(LINEAR_ATTN_COUNT, TILE_NUMBER, TILE_WIDTH).transpose(1, 0, 2)
    terms = lax.map(lambda pieces: block_terms(*pieces), (queries, keys_in, values, douts, decay))
    same_doc = (doc_block[1:] == doc_block[:-1]).astype(jnp.float32)
    follows = jnp.concatenate([jnp.zeros((1,), jnp.float32), same_doc])
    precedes = jnp.concatenate([same_doc, jnp.zeros((1,), jnp.float32)])
    zero_state = jnp.zeros((LINEAR_ATTN_COUNT, HD, HD), jnp.float32)

    def link(carried, pieces):
        state_now, total_now, joined = pieces
        entering = joined * carried
        return state_now + jnp.exp(total_now)[:, None, None] * entering, entering

    unused_one, into_all = lax.scan(link, zero_state, (terms[6], terms[5], follows))
    unused_two, back_all = lax.scan(link, zero_state, (terms[7], terms[5], precedes), reverse=True)
    grads = lax.map(lambda pieces: finish(*pieces), (terms, keys_in, values, douts, into_all, back_all))
    return tuple(grad.reshape(SEQ, LINEAR_ATTN_COUNT, HD) for grad in grads)


def attention_grads(att_q, att_k, att_v, att_dout, doc_block):
    scale = HD ** -0.5
    window = MOST_BLK * TILE_WIDTH
    margin = window - TILE_WIDTH
    keys_pad = jnp.concatenate([jnp.zeros((margin, HD), jnp.float32), att_k.astype(jnp.float32)])
    values_pad = jnp.concatenate([jnp.zeros((margin, HD), jnp.float32), att_v.astype(jnp.float32)])
    token_doc = jnp.repeat(doc_block, TILE_WIDTH)
    key_doc = jnp.concatenate([jnp.full((margin,), -1, jnp.int32), token_doc])
    offsets_q = jnp.arange(TILE_WIDTH, dtype=jnp.int32)
    offsets_k = jnp.arange(window, dtype=jnp.int32)

    def one_block(carried, index):
        grad_keys, grad_values = carried
        begin = (index * TILE_WIDTH).astype(jnp.int32)
        queries = lax.dynamic_slice_in_dim(att_q, begin, TILE_WIDTH).astype(jnp.float32)
        douts = lax.dynamic_slice_in_dim(att_dout, begin, TILE_WIDTH).astype(jnp.float32)
        near_keys = lax.dynamic_slice_in_dim(keys_pad, begin, window)
        near_values = lax.dynamic_slice_in_dim(values_pad, begin, window)
        near_doc = lax.dynamic_slice_in_dim(key_doc, begin, window)
        query_doc = lax.dynamic_slice_in_dim(token_doc, begin, TILE_WIDTH)
        query_pos = begin + offsets_q
        key_pos = begin - margin + offsets_k
        visible = (query_doc[:, None] == near_doc[None, :]) & (key_pos[None, :] <= query_pos[:, None])
        scores = jnp.einsum("thd,sd->hts", queries, near_keys) * scale
        scores = jnp.where(visible[None], scores, NEG)
        row_max = jnp.max(scores, axis=2)
        plain = jnp.where(visible[None], jnp.exp(scores - row_max[:, :, None]), 0.0)
        row_sum = jnp.sum(plain, axis=2)
        grad_probs = jnp.einsum("thd,sd->hts", douts, near_values)
        lse = row_max + jnp.log(row_sum)
        delta = jnp.sum(plain * grad_probs, axis=2) / row_sum
        probs = jnp.where(visible[None], jnp.exp(scores - lse[:, :, None]), 0.0)
        grad_scores = probs * (grad_probs - delta[:, :, None])
        probs_b = rounded(probs)
        grad_b = rounded(grad_scores)
        block_query = jnp.einsum("hts,sd->thd", grad_b, near_keys) * scale
        part_key = jnp.einsum("hts,thd->sd", grad_b, queries)
        part_value = jnp.einsum("hts,thd->sd", probs_b, douts)
        grad_keys = lax.dynamic_update_slice_in_dim(grad_keys, lax.dynamic_slice_in_dim(grad_keys, begin, window) + part_key, begin, 0)
        grad_values = lax.dynamic_update_slice_in_dim(grad_values, lax.dynamic_slice_in_dim(grad_values, begin, window) + part_value, begin, 0)
        return (grad_keys, grad_values), block_query.astype(jnp.bfloat16)

    start = (jnp.zeros((margin + SEQ, HD), jnp.float32), jnp.zeros((margin + SEQ, HD), jnp.float32))
    finals, blocks = lax.scan(one_block, start, jnp.arange(TILE_NUMBER, dtype=jnp.int32))
    att_dq = blocks.reshape(SEQ, QHEADS, HD)
    att_dk = (finals[0][margin:] * scale).astype(jnp.bfloat16)
    att_dv = finals[1][margin:].astype(jnp.bfloat16)
    return att_dq, att_dk, att_dv


def reference(lin_q, lin_k, lin_v, lin_dout, lin_decay, att_q, att_k, att_v, att_dout, doc_block):
    lin_out = lightning_grads(lin_q, lin_k, lin_v, lin_dout, lin_decay, doc_block)
    att_out = attention_grads(att_q, att_k, att_v, att_dout, doc_block)
    return (lin_out[0], lin_out[1], lin_out[2], att_out[0], att_out[1], att_out[2])
```

```python
import functools
import math

import jax
import jax.numpy as jnp
from jax import lax
from jax.experimental import pallas as pl
from jax.experimental.pallas import tpu as pltpu
from jax.sharding import PartitionSpec as P

TILE = 256
MOST = 12
NEG = -1e30
MESH = pl.DeviceIdType.MESH
F32 = jnp.float32
BF16 = jnp.bfloat16


def dot_nn(a, b):
    return lax.dot_general(a, b, (((1,), (0,)), ((), ())), preferred_element_type=F32)


def dot_nt(a, b):
    return lax.dot_general(a, b, (((1,), (1,)), ((), ())), preferred_element_type=F32)


def dot_tn(a, b):
    return lax.dot_general(a, b, (((0,), (0,)), ((), ())), preferred_element_type=F32)


def split(x):
    high = x.astype(BF16)
    return high, (x - high.astype(F32)).astype(BF16)


def greet(me, core, count, reach):
    barrier = pltpu.get_barrier_semaphore()
    pl.semaphore_signal(barrier, inc=1, device_id={"head": 1 - core}, device_id_type=MESH)
    for step in range(1, reach + 1):

        @pl.when(me + step < count)
        def _():
            pl.semaphore_signal(barrier, inc=1, device_id={"ctx": me + step}, device_id_type=MESH)

        @pl.when(me - step >= 0)
        def _():
            pl.semaphore_signal(barrier, inc=1, device_id={"ctx": me - step}, device_id_type=MESH)

    pl.semaphore_wait(
        barrier, 1 + jnp.minimum(me, reach) + jnp.minimum(count - 1 - me, reach)
    )


def lightning_kernel(
    count, reach, heads, nblocks,
    doc, lq, lk, lv, ld, dec, att_k, att_v,
    dq, dk, dv, kall, vall,
    wide, parts, grads, states,
    send_l, recv_l, send_r, recv_r, echo_l, land_l, echo_r, land_r,
    own_sem, kv_send, kv_recv, pair_send, pair_recv, st_send, st_recv,
):
    me = lax.axis_index("ctx")
    core = lax.axis_index("head")
    length = nblocks * TILE
    half = length // 2
    width = lq.shape[1]
    rows = TILE * heads
    greet(me, core, count, reach)

    pairs = ((att_k, kall), (att_v, vall))
    start = pl.multiple_of(core * half, half)

    def kv_copy(which, step):
        source, target = pairs[which]
        place = pl.multiple_of((reach - step) * length + core * half, half)
        return pltpu.make_async_remote_copy(
            src_ref=source.at[pl.ds(start, half)],
            dst_ref=target.at[pl.ds(place, half)],
            send_sem=kv_send.at[which, step - 1],
            recv_sem=kv_recv.at[which, step - 1],
            device_id={"ctx": me + step},
            device_id_type=MESH,
        )

    def pair_copy(which, step):
        target = pairs[which][1]
        place = pl.multiple_of((reach - step) * length + core * half, half)
        return pltpu.make_async_remote_copy(
            src_ref=target.at[pl.ds(place, half)],
            dst_ref=target.at[pl.ds(place, half)],
            send_sem=pair_send.at[which, step - 1],
            recv_sem=pair_recv.at[which, step - 1],
            device_id={"head": 1 - core},
            device_id_type=MESH,
        )

    for step in range(1, reach + 1):

        @pl.when(me + step < count)
        def _():
            kv_copy(0, step).start()
            kv_copy(1, step).start()

    own = [
        pltpu.make_async_copy(
            pairs[which][0], pairs[which][1].at[pl.ds(reach * length, length)], own_sem.at[which]
        )
        for which in range(2)
    ]
    own[0].start()
    own[1].start()

    t_sub = lax.broadcasted_iota(jnp.int32, (TILE, TILE), 0)
    t_lane = lax.broadcasted_iota(jnp.int32, (TILE, TILE), 1)
    upper = (t_sub <= t_lane).astype(F32)
    lower = (t_sub >= t_lane).astype(F32)

    def link(at_one, at_two):
        one = jnp.clip(at_one, 0, count * nblocks - 1)
        two = jnp.clip(at_two, 0, count * nblocks - 1)
        inside = jnp.logical_and(at_one >= 0, at_two < count * nblocks)
        same = jnp.logical_and(doc[one] == doc[two], inside)
        return jnp.where(same, 1.0, 0.0).astype(F32)

    follows = [link(me * nblocks + b - 1, me * nblocks + b) for b in range(nblocks)]
    precedes = [link(me * nblocks + b, me * nblocks + b + 1) for b in range(nblocks)]

    cum_row, cum_col = [], []
    for b in range(nblocks):
        piece = dec[:, b * TILE : (b + 1) * TILE]
        cum_row.append(
            lax.dot_general(
                piece, upper, (((1,), (0,)), ((), ())),
                preferred_element_type=F32, precision=lax.Precision.HIGHEST,
            )
        )
        cum_col.append(
            lax.dot_general(
                lower, piece, (((1,), (1,)), ((), ())),
                preferred_element_type=F32, precision=lax.Precision.HIGHEST,
            )
        )

    def head_terms(b, h):
        row = cum_row[b][h : h + 1, :]
        col = cum_col[b][:, h : h + 1]
        total = col[TILE - 1 : TILE, :]
        return row, col, total

    for b in range(nblocks):
        for a, ref in enumerate((lq, lk, lv, ld)):
            wide[a] = ref[b * rows : (b + 1) * rows, :].astype(F32)
        for h in range(heads):
            row, col, total = head_terms(b, h)
            picked = [wide[a, pl.ds(h, TILE, stride=heads), :] for a in range(4)]
            for a in range(4):
                parts[a, b, h] = picked[a].astype(BF16)
            key_high, key_low = split((picked[1] * jnp.exp(total - col)).T)
            value = picked[2].astype(BF16)
            states[0, b, h] = dot_nn(key_high, value) + dot_nn(key_low, value)
            query_high, query_low = split((picked[0] * jnp.exp(col)).T)
            dout = picked[3].astype(BF16)
            states[1, b, h] = dot_nn(query_high, dout) + dot_nn(query_low, dout)

    for h in range(heads):
        keep = [jnp.exp(head_terms(b, h)[2]) for b in range(nblocks)]
        total_l = states[0, 0, h]
        mult_l = keep[0] * follows[0]
        for b in range(1, nblocks):
            total_l = states[0, b, h] + keep[b] * follows[b] * total_l
            mult_l = mult_l * keep[b] * follows[b]
        total_r = states[1, nblocks - 1, h]
        mult_r = keep[nblocks - 1] * precedes[nblocks - 1]
        for b in reversed(range(nblocks - 1)):
            total_r = states[1, b, h] + keep[b] * precedes[b] * total_r
            mult_r = mult_r * keep[b] * precedes[b]
        send_l[h, 0:width, :] = total_l
        send_r[h, 0:width, :] = total_r
        send_l[h, width : width + 8, :] = jnp.broadcast_to(mult_l, (8, width))
        send_r[h, width : width + 8, :] = jnp.broadcast_to(mult_r, (8, width))

    def state_copy(side, step):
        return pltpu.make_async_remote_copy(
            src_ref=(send_l, send_r)[side],
            dst_ref=(recv_l, recv_r)[side].at[step - 1],
            send_sem=st_send.at[side, step - 1],
            recv_sem=st_recv.at[side, step - 1],
            device_id={"ctx": me + step if side == 0 else me - step},
            device_id_type=MESH,
        )

    def echo_copy(side):
        return pltpu.make_async_remote_copy(
            src_ref=(echo_l, echo_r)[side],
            dst_ref=(land_l, land_r)[side],
            send_sem=st_send.at[side, 3],
            recv_sem=st_recv.at[side, 3],
            device_id={"ctx": me + 3 if side == 0 else me - 3},
            device_id_type=MESH,
        )

    for step in (1, 2, 3):

        @pl.when(me + step < count)
        def _():
            state_copy(0, step).start()

        @pl.when(me - step >= 0)
        def _():
            state_copy(1, step).start()

        @pl.when(me - step < 0)
        def _():
            recv_l[step - 1] = jnp.zeros(recv_l.shape[1:], F32)

        @pl.when(me + step >= count)
        def _():
            recv_r[step - 1] = jnp.zeros(recv_r.shape[1:], F32)

    @pl.when(me - 3 < 0)
    def _():
        land_l[...] = jnp.zeros(land_l.shape, F32)

    @pl.when(me + 3 >= count)
    def _():
        land_r[...] = jnp.zeros(land_r.shape, F32)

    def within(b):
        for h in range(heads):
            row, col, total = head_terms(b, h)
            query, key, value, dout = (parts[a, b, h] for a in range(4))
            seen = t_sub <= t_lane
            weight = jnp.where(seen, jnp.exp(jnp.where(seen, row - col, 0.0)), 0.0)
            left = (dot_nt(value, dout) * weight).astype(BF16)
            right = (dot_nt(key, query) * weight).astype(BF16)
            at = pl.ds(b * rows + h, TILE, stride=heads)
            grads[0, at, :] = dot_tn(left, key)
            grads[1, at, :] = dot_nn(left, query)
            grads[2, at, :] = dot_nn(right, dout)

    for b in range(nblocks):
        within(b)

    def wait_states(step):
        @pl.when(me - step >= 0)
        def _():
            state_copy(0, step).wait_recv()

        @pl.when(me + step < count)
        def _():
            state_copy(1, step).wait_recv()

    for step in (1, 2, 3):
        wait_states(step)
    for recv, echo in ((recv_l, echo_l), (recv_r, echo_r)):
        for h in range(heads):
            one = recv[0, h, width : width + 1, :]
            two = recv[1, h, width : width + 1, :]
            echo[h] = recv[0, h, 0:width, :] + one * (
                recv[1, h, 0:width, :] + two * recv[2, h, 0:width, :]
            )

    @pl.when(me + 3 < count)
    def _():
        echo_copy(0).start()

    @pl.when(me - 3 >= 0)
    def _():
        echo_copy(1).start()

    def pass_on(step):
        @pl.when(me - step >= 0)
        def _():
            for which in range(2):
                kv_copy(which, step).wait_recv()
                pair_copy(which, step).start()

    pass_on(1)
    pass_on(2)

    @pl.when(me - 3 >= 0)
    def _():
        echo_copy(0).wait_recv()

    @pl.when(me + 3 < count)
    def _():
        echo_copy(1).wait_recv()

    for h in range(heads):
        keep = [jnp.exp(head_terms(b, h)[2]) for b in range(nblocks)]
        span_l = recv_l[0, h, width : width + 1, :] * recv_l[1, h, width : width + 1, :]
        span_l = span_l * recv_l[2, h, width : width + 1, :]
        span_r = recv_r[0, h, width : width + 1, :] * recv_r[1, h, width : width + 1, :]
        span_r = span_r * recv_r[2, h, width : width + 1, :]
        state = echo_l[h] + span_l * land_l[h]
        into = []
        for b in range(nblocks):
            into.append(follows[b] * state)
            state = states[0, b, h] + keep[b] * into[b]
        state = echo_r[h] + span_r * land_r[h]
        back = [None] * nblocks
        for b in reversed(range(nblocks)):
            back[b] = precedes[b] * state
            state = states[1, b, h] + keep[b] * back[b]
        for b in range(nblocks):
            row, col, total = head_terms(b, h)
            query, key, value, dout = (parts[a, b, h] for a in range(4))
            head_decay = jnp.exp(col)
            tail_decay = jnp.exp(total - col)
            into_high, into_low = split(into[b])
            back_high, back_low = split(back[b])
            at = pl.ds(b * rows + h, TILE, stride=heads)
            grads[0, at, :] = grads[0, at, :] + head_decay * (
                dot_nt(dout, into_high) + dot_nt(dout, into_low)
            )
            grads[1, at, :] = grads[1, at, :] + tail_decay * (
                dot_nt(value, back_high) + dot_nt(value, back_low)
            )
            grads[2, at, :] = grads[2, at, :] + tail_decay * (
                dot_nn(key, back_high) + dot_nn(key, back_low)
            )
    dq[...] = grads[0].astype(BF16)
    dk[...] = grads[1].astype(BF16)
    dv[...] = grads[2].astype(BF16)

    for step in range(3, reach + 1):
        pass_on(step)
    for step in range(1, reach + 1):

        @pl.when(me - step >= 0)
        def _():
            for which in range(2):
                pair_copy(which, step).wait()

        @pl.when(me + step < count)
        def _():
            for which in range(2):
                kv_copy(which, step).wait_send()

    for step in (1, 2, 3):

        @pl.when(me + step < count)
        def _():
            state_copy(0, step).wait_send()

        @pl.when(me - step >= 0)
        def _():
            state_copy(1, step).wait_send()

    @pl.when(me + 3 < count)
    def _():
        echo_copy(0).wait_send()

    @pl.when(me - 3 >= 0)
    def _():
        echo_copy(1).wait_send()

    own[0].wait()
    own[1].wait()


def attention_kernel(
    nblocks, reach, heads, chunk, spot,
    q, dout, keys_in, values, dq, dkey, dvalue, scores, probs_grad, flipped,
):
    index = pl.program_id(0)
    width = q.shape[1]
    scale = width ** (-0.5)
    log2e = math.log2(math.e)
    factor = scale * log2e
    total_blocks = keys_in.shape[0] // TILE

    @pl.when(index == 0)
    def _():
        dkey[...] = jnp.zeros(dkey.shape, F32)
        dvalue[...] = jnp.zeros(dvalue.shape, F32)

        @pl.loop(0, total_blocks)
        def _(j):
            at = pl.ds(pl.multiple_of(j * TILE, TILE), TILE)
            flipped[j] = keys_in[at, :].astype(F32).T.astype(BF16)

    per_block = TILE * heads // chunk
    block = index // per_block
    diag = reach * nblocks + block
    first = diag + 1 - spot[block]
    queries = q[...]
    douts = dout[...]

    token = (lax.broadcasted_iota(jnp.int32, (TILE, chunk), 1) + (index % per_block) * chunk) // heads
    seen = lax.broadcasted_iota(jnp.int32, (TILE, chunk), 0) <= token

    def rows_of(j):
        return pl.ds(pl.multiple_of(j * TILE, TILE), TILE)

    def folded(x, op):
        return op(x.reshape(TILE // 8, 8, chunk), axis=0)

    s = jnp.where(seen, dot_nt(keys_in[rows_of(diag), :], queries), NEG)
    scores[diag] = s

    def find_max(j, top):
        s = dot_nt(keys_in[rows_of(j), :], queries)
        scores[j] = s
        return jnp.maximum(top, folded(s, jnp.max))

    top = lax.fori_loop(first, diag, find_max, folded(s, jnp.max))
    top = jnp.max(top, axis=0, keepdims=True) * factor

    def sums(j, carried):
        amount, weighted = carried
        p = jnp.exp2(scores[j] * factor - top)
        g = dot_nt(values[rows_of(j), :], douts)
        scores[j] = p
        probs_grad[j] = g
        return amount + folded(p, jnp.sum), weighted + folded(p * g, jnp.sum)

    zero = jnp.zeros((8, chunk), F32)
    amount, weighted = lax.fori_loop(first, diag + 1, sums, (zero, zero))
    inverse = 1.0 / jnp.sum(amount, axis=0, keepdims=True)
    delta = jnp.sum(weighted, axis=0, keepdims=True) * inverse

    def grads(j, acc):
        p = scores[j] * inverse
        g = p * (probs_grad[j] - delta)
        p = p.astype(BF16)
        g = g.astype(BF16)
        at = rows_of(j)
        dvalue[at, :] += dot_nn(p, douts)
        dkey[at, :] += dot_nn(g, queries)
        return acc + dot_nn(flipped[j], g)

    acc = lax.fori_loop(first, diag + 1, grads, jnp.zeros((width, chunk), F32))
    dq[...] = (acc.T * scale).astype(BF16)


def reduce_kernel(
    count, reach, length, dkey, dvalue, dk, dv, paired, out, inbox,
    pair_send, pair_recv, send_sem, recv_sem,
):
    me = lax.axis_index("ctx")
    core = lax.axis_index("head")
    half = length // 2
    scale = dkey.shape[1] ** (-0.5)
    greet(me, core, count, reach)
    sources = (dkey, dvalue)

    def pair_copy(which, step):
        place = pl.multiple_of((reach - step) * length + (1 - core) * half, half)
        return pltpu.make_async_remote_copy(
            src_ref=sources[which].at[pl.ds(place, half)],
            dst_ref=paired.at[which, step],
            send_sem=pair_send.at[which, step],
            recv_sem=pair_recv.at[which, step],
            device_id={"head": 1 - core},
            device_id_type=MESH,
        )

    def home_copy(step):
        return pltpu.make_async_remote_copy(
            src_ref=out.at[step - 1],
            dst_ref=inbox.at[step - 1],
            send_sem=send_sem.at[step - 1],
            recv_sem=recv_sem.at[step - 1],
            device_id={"ctx": me - step},
            device_id_type=MESH,
        )

    order = list(range(reach, -1, -1))
    for step in order:
        pair_copy(0, step).start()
        pair_copy(1, step).start()

    def mine(which, step):
        place = pl.multiple_of((reach - step) * length + core * half, half)
        return sources[which][pl.ds(place, half), :] + paired[which, step]

    for step in order:
        for which in range(2):
            pair_copy(which, step).wait_recv()
        if step > 0:
            for which in range(2):
                out[step - 1, which] = mine(which, step).astype(BF16)

            @pl.when(me - step >= 0)
            def _():
                home_copy(step).start()

        if step > 0:

            @pl.when(me + step >= count)
            def _():
                inbox[step - 1] = jnp.zeros(inbox.shape[1:], BF16)

    paired[0, 0] = mine(0, 0)
    paired[1, 0] = mine(1, 0)
    for step in range(1, reach + 1):

        @pl.when(me + step < count)
        def _():
            home_copy(step).wait_recv()

        for which in range(2):
            paired[which, 0] += inbox[step - 1, which].astype(F32)
    dk[...] = (paired[0, 0] * scale).astype(BF16)
    dv[...] = paired[1, 0].astype(BF16)
    for step in order:
        pair_copy(0, step).wait_send()
        pair_copy(1, step).wait_send()
        if step > 0:

            @pl.when(me - step >= 0)
            def _():
                home_copy(step).wait_send()


def shards(count, lin_q, lin_k, lin_v, lin_dout, lin_decay, att_q, att_k, att_v, att_dout, doc_block):
    length, heads, width = lin_q.shape
    nblocks = length // TILE
    reach = -(-(MOST - 1) // nblocks)
    half = length // 2
    flat = lambda x: x.reshape(length * heads, width)
    shape = jax.ShapeDtypeStruct
    vmem = pl.BlockSpec(memory_space=pltpu.VMEM)
    smem = pl.BlockSpec(memory_space=pltpu.SMEM)
    anywhere = pl.BlockSpec(memory_space=pl.ANY)
    rows = length * heads
    window = (reach + 1) * length
    state = (heads, width, width)
    packet = (heads, width + 8, width)
    dma = pltpu.SemaphoreType.DMA
    lin_dq, lin_dk, lin_dv, kall, vall = pl.pallas_call(
        functools.partial(lightning_kernel, count, reach, heads, nblocks),
        out_shape=[shape((rows, width), BF16)] * 3 + [shape((window, width), BF16)] * 2,
        in_specs=[smem] + [vmem] * 5 + [anywhere] * 2,
        out_specs=[vmem] * 3 + [anywhere] * 2,
        scratch_shapes=[
            pltpu.VMEM((4, TILE * heads, width), F32),
            pltpu.VMEM((4, nblocks, heads, TILE, width), BF16),
            pltpu.VMEM((3, rows, width), F32),
            pltpu.VMEM((2, nblocks) + state, F32),
            pltpu.VMEM(packet, F32),
            pltpu.VMEM((3,) + packet, F32),
            pltpu.VMEM(packet, F32),
            pltpu.VMEM((3,) + packet, F32),
            pltpu.VMEM(state, F32),
            pltpu.VMEM(state, F32),
            pltpu.VMEM(state, F32),
            pltpu.VMEM(state, F32),
            dma((2,)),
            dma((2, reach)),
            dma((2, reach)),
            dma((2, reach)),
            dma((2, reach)),
            dma((2, 4)),
            dma((2, 4)),
        ],
        compiler_params=pltpu.CompilerParams(
            collective_id=0, has_side_effects=True, vmem_limit_bytes=40 * 1024 * 1024
        ),
        name="lightning",
    )(doc_block, flat(lin_q), flat(lin_k), flat(lin_v), flat(lin_dout), lin_decay, att_k, att_v)

    me = lax.axis_index("ctx")
    here = lax.dynamic_slice_in_dim(doc_block, me * nblocks, nblocks)
    at = me * nblocks + jnp.arange(nblocks, dtype=jnp.int32)
    before = jnp.sum((doc_block[None, :] < here[:, None]).astype(jnp.int32), axis=1)
    spot = at - before + 1
    chunk = 512
    att_dq, dkey, dvalue = pl.pallas_call(
        functools.partial(attention_kernel, nblocks, reach, heads, chunk),
        grid_spec=pltpu.PrefetchScalarGridSpec(
            num_scalar_prefetch=1,
            grid=(rows // chunk,),
            in_specs=[
                pl.BlockSpec((chunk, width), lambda i, s: (i, 0)),
                pl.BlockSpec((chunk, width), lambda i, s: (i, 0)),
                pl.BlockSpec((window, width), lambda i, s: (0, 0)),
                pl.BlockSpec((window, width), lambda i, s: (0, 0)),
            ],
            out_specs=[
                pl.BlockSpec((chunk, width), lambda i, s: (i, 0)),
                pl.BlockSpec((window, width), lambda i, s: (0, 0)),
                pl.BlockSpec((window, width), lambda i, s: (0, 0)),
            ],
            scratch_shapes=[
                pltpu.VMEM((window // TILE, TILE, chunk), F32),
                pltpu.VMEM((window // TILE, TILE, chunk), F32),
                pltpu.VMEM((window // TILE, width, TILE), BF16),
            ],
        ),
        out_shape=[
            shape((rows, width), BF16),
            shape((window, width), F32),
            shape((window, width), F32),
        ],
        compiler_params=pltpu.CompilerParams(vmem_limit_bytes=50 * 1024 * 1024),
        name="attention",
    )(spot, flat(att_q), flat(att_dout), kall, vall)

    att_dk, att_dv = pl.pallas_call(
        functools.partial(reduce_kernel, count, reach, length),
        out_shape=[shape((half, width), BF16)] * 2,
        in_specs=[vmem] * 2,
        out_specs=[vmem] * 2,
        scratch_shapes=[
            pltpu.VMEM((2, reach + 1, half, width), F32),
            pltpu.VMEM((reach, 2, half, width), BF16),
            pltpu.VMEM((reach, 2, half, width), BF16),
            dma((2, reach + 1)),
            dma((2, reach + 1)),
            dma((reach,)),
            dma((reach,)),
        ],
        compiler_params=pltpu.CompilerParams(
            collective_id=1, has_side_effects=True, vmem_limit_bytes=40 * 1024 * 1024
        ),
        name="reduce",
    )(dkey, dvalue)
    full = lambda x: x.reshape(length, heads, width)
    return (full(lin_dq), full(lin_dk), full(lin_dv), full(att_dq), att_dk, att_dv)


def solution(mesh):
    return jax.shard_map(
        functools.partial(shards, mesh.shape["ctx"]),
        mesh=mesh,
        in_specs=(
            P("ctx", "head", None),
            P("ctx", "head", None),
            P("ctx", "head", None),
            P("ctx", "head", None),
            P("head", "ctx"),
            P("ctx", "head", None),
            P("ctx", None),
            P("ctx", None),
            P("ctx", "head", None),
            P(),
        ),
        out_specs=(
            P("ctx", "head", None),
            P("ctx", "head", None),
            P("ctx", "head", None),
            P("ctx", "head", None),
            P(("ctx", "head"), None),
            P(("ctx", "head"), None),
        ),
        check_vma=False,
    )
```

```python
import functools
import math

import jax
import jax.numpy as jnp
from jax import lax
from jax.experimental import pallas as pl
from jax.experimental.pallas import tpu as pltpu
from jax.sharding import PartitionSpec as P

TILE = 256
MOST = 12
NEG = -1e30
MESH = pl.DeviceIdType.MESH
F32 = jnp.float32
BF16 = jnp.bfloat16
SHAPE = jax.ShapeDtypeStruct
DMA = pltpu.SemaphoreType.DMA
IN_VMEM = pl.BlockSpec(memory_space=pltpu.VMEM)
IN_SMEM = pl.BlockSpec(memory_space=pltpu.SMEM)
ANYWHERE = pl.BlockSpec(memory_space=pl.ANY)
VMEM_LIMIT = 56 * 1024 * 1024


def dot_nn(a, b):
    return lax.dot_general(a, b, (((1,), (0,)), ((), ())), preferred_element_type=F32)


def dot_nt(a, b):
    return lax.dot_general(a, b, (((1,), (1,)), ((), ())), preferred_element_type=F32)


def dot_tn(a, b):
    return lax.dot_general(a, b, (((0,), (0,)), ((), ())), preferred_element_type=F32)


def split(x):
    high = x.astype(BF16)
    return high, (x - high.astype(F32)).astype(BF16)


def greet(me, core, count, reach):
    barrier = pltpu.get_barrier_semaphore()
    pl.semaphore_signal(barrier, inc=1, device_id={"head": 1 - core}, device_id_type=MESH)
    for step in range(1, reach + 1):

        @pl.when(me + step < count)
        def _():
            pl.semaphore_signal(barrier, inc=1, device_id={"ctx": me + step}, device_id_type=MESH)

        @pl.when(me - step >= 0)
        def _():
            pl.semaphore_signal(barrier, inc=1, device_id={"ctx": me - step}, device_id_type=MESH)

    pl.semaphore_wait(
        barrier, 1 + jnp.minimum(me, reach) + jnp.minimum(count - 1 - me, reach)
    )


def decay_terms(me, count, nblocks, doc, dec):
    t_sub = lax.broadcasted_iota(jnp.int32, (TILE, TILE), 0)
    t_lane = lax.broadcasted_iota(jnp.int32, (TILE, TILE), 1)
    upper = (t_sub <= t_lane).astype(F32)
    lower = (t_sub >= t_lane).astype(F32)

    def link(at_one, at_two):
        one = jnp.clip(at_one, 0, count * nblocks - 1)
        two = jnp.clip(at_two, 0, count * nblocks - 1)
        inside = jnp.logical_and(at_one >= 0, at_two < count * nblocks)
        same = jnp.logical_and(doc[one] == doc[two], inside)
        return jnp.where(same, 1.0, 0.0).astype(F32)

    follows = [link(me * nblocks + b - 1, me * nblocks + b) for b in range(nblocks)]
    precedes = [link(me * nblocks + b, me * nblocks + b + 1) for b in range(nblocks)]

    cum_row, cum_col = [], []
    for b in range(nblocks):
        piece = dec[:, b * TILE : (b + 1) * TILE]
        cum_row.append(
            lax.dot_general(
                piece, upper, (((1,), (0,)), ((), ())),
                preferred_element_type=F32, precision=lax.Precision.HIGHEST,
            )
        )
        cum_col.append(
            lax.dot_general(
                lower, piece, (((1,), (1,)), ((), ())),
                preferred_element_type=F32, precision=lax.Precision.HIGHEST,
            )
        )

    def head_terms(b, h):
        row = cum_row[b][h : h + 1, :]
        col = cum_col[b][:, h : h + 1]
        total = col[TILE - 1 : TILE, :]
        return row, col, total

    return follows, precedes, head_terms, t_sub, t_lane


def lightning_kernel(
    count, reach, heads, nblocks,
    doc, lq, lk, lv, ld, dec_in, att_k, att_v,
    send_l, send_r, parts, states, kall, vall,
    wide, raw, dec, raw_sem, own_sem, kv_send, kv_recv, pair_send, pair_recv,
):
    me = lax.axis_index("ctx")
    core = lax.axis_index("head")
    length = nblocks * TILE
    half = length // 2
    width = lq.shape[1]
    rows = TILE * heads
    loads = [
        pltpu.make_async_copy(ref, raw.at[a], raw_sem.at[a])
        for a, ref in enumerate((lq, lk, lv, ld))
    ]
    loads.append(pltpu.make_async_copy(dec_in, dec, raw_sem.at[4]))
    for load in loads:
        load.start()
    greet(me, core, count, reach)

    pairs = ((att_k, kall), (att_v, vall))
    start = pl.multiple_of(core * half, half)

    def kv_copy(which, step):
        source, target = pairs[which]
        place = pl.multiple_of((reach - step) * length + core * half, half)
        return pltpu.make_async_remote_copy(
            src_ref=source.at[pl.ds(start, half)],
            dst_ref=target.at[pl.ds(place, half)],
            send_sem=kv_send.at[which, step - 1],
            recv_sem=kv_recv.at[which, step - 1],
            device_id={"ctx": me + step},
            device_id_type=MESH,
        )

    def pair_copy(which, step):
        target = pairs[which][1]
        place = pl.multiple_of((reach - step) * length + core * half, half)
        return pltpu.make_async_remote_copy(
            src_ref=target.at[pl.ds(place, half)],
            dst_ref=target.at[pl.ds(place, half)],
            send_sem=pair_send.at[which, step - 1],
            recv_sem=pair_recv.at[which, step - 1],
            device_id={"head": 1 - core},
            device_id_type=MESH,
        )

    for step in range(1, reach + 1):

        @pl.when(me + step < count)
        def _():
            kv_copy(0, step).start()
            kv_copy(1, step).start()

    own = [
        pltpu.make_async_copy(
            pairs[which][0], pairs[which][1].at[pl.ds(reach * length, length)], own_sem.at[which]
        )
        for which in range(2)
    ]
    own[0].start()
    own[1].start()

    for load in loads:
        load.wait()
    follows, precedes, head_terms, _, _ = decay_terms(me, count, nblocks, doc, dec)

    for b in range(nblocks):
        for a in range(4):
            wide[a] = raw[a, b * rows : (b + 1) * rows, :].astype(F32)
        for h in range(heads):
            row, col, total = head_terms(b, h)
            picked = [wide[a, pl.ds(h, TILE, stride=heads), :] for a in range(4)]
            for a in range(4):
                parts[a, b, h] = picked[a].astype(BF16)
            key_high, key_low = split((picked[1] * jnp.exp(total - col)).T)
            value = picked[2].astype(BF16)
            states[0, b, h] = dot_nn(key_high, value) + dot_nn(key_low, value)
            query_high, query_low = split((picked[0] * jnp.exp(col)).T)
            dout = picked[3].astype(BF16)
            states[1, b, h] = dot_nn(query_high, dout) + dot_nn(query_low, dout)

    for h in range(heads):
        keep = [jnp.exp(head_terms(b, h)[2]) for b in range(nblocks)]
        total_l = states[0, 0, h]
        mult_l = keep[0] * follows[0]
        for b in range(1, nblocks):
            total_l = states[0, b, h] + keep[b] * follows[b] * total_l
            mult_l = mult_l * keep[b] * follows[b]
        total_r = states[1, nblocks - 1, h]
        mult_r = keep[nblocks - 1] * precedes[nblocks - 1]
        for b in reversed(range(nblocks - 1)):
            total_r = states[1, b, h] + keep[b] * precedes[b] * total_r
            mult_r = mult_r * keep[b] * precedes[b]
        for send, total, mult in ((send_l, total_l, mult_l), (send_r, total_r, mult_r)):
            high, low = split(jnp.broadcast_to(mult, (16, width)))
            send[h, 0:width, :] = total.astype(BF16)
            send[h, width : width + 16, :] = high
            send[h, width + 16 : width + 32, :] = low

    def pass_on(step):
        @pl.when(me - step >= 0)
        def _():
            for which in range(2):
                kv_copy(which, step).wait_recv()
                pair_copy(which, step).start()

    for step in range(1, reach + 1):
        pass_on(step)
    for step in range(1, reach + 1):

        @pl.when(me - step >= 0)
        def _():
            for which in range(2):
                pair_copy(which, step).wait()

        @pl.when(me + step < count)
        def _():
            for which in range(2):
                kv_copy(which, step).wait_send()

    own[0].wait()
    own[1].wait()


def attention_kernel(
    nblocks, reach, heads, chunk, spot,
    q, dout, keys_in, values, dq, dkey, dvalue, scores, probs_grad, flipped,
):
    index = pl.program_id(0)
    width = q.shape[1]
    scale = width ** (-0.5)
    log2e = math.log2(math.e)
    factor = scale * log2e
    total_blocks = keys_in.shape[0] // TILE

    @pl.when(index == 0)
    def _():
        dkey[...] = jnp.zeros(dkey.shape, F32)
        dvalue[...] = jnp.zeros(dvalue.shape, F32)

        @pl.loop(0, total_blocks)
        def _(j):
            at = pl.ds(pl.multiple_of(j * TILE, TILE), TILE)
            flipped[j] = keys_in[at, :].astype(F32).T.astype(BF16)

    per_block = TILE * heads // chunk
    block = index // per_block
    diag = reach * nblocks + block
    first = diag + 1 - spot[block]
    queries = q[...]
    douts = dout[...]

    token = (lax.broadcasted_iota(jnp.int32, (TILE, chunk), 1) + (index % per_block) * chunk) // heads
    seen = lax.broadcasted_iota(jnp.int32, (TILE, chunk), 0) <= token

    def rows_of(j):
        return pl.ds(pl.multiple_of(j * TILE, TILE), TILE)

    def folded(x, op):
        return op(x.reshape(TILE // 8, 8, chunk), axis=0)

    s = jnp.where(seen, dot_nt(keys_in[rows_of(diag), :], queries), NEG)
    scores[diag] = s

    def find_max(j, top):
        s = dot_nt(keys_in[rows_of(j), :], queries)
        scores[j] = s
        return jnp.maximum(top, folded(s, jnp.max))

    top = lax.fori_loop(first, diag, find_max, folded(s, jnp.max))
    top = jnp.max(top, axis=0, keepdims=True) * factor

    def sums(j, carried):
        amount, weighted = carried
        p = jnp.exp2(scores[j] * factor - top)
        g = dot_nt(values[rows_of(j), :], douts)
        scores[j] = p
        probs_grad[j] = g
        return amount + folded(p, jnp.sum), weighted + folded(p * g, jnp.sum)

    zero = jnp.zeros((8, chunk), F32)
    amount, weighted = lax.fori_loop(first, diag + 1, sums, (zero, zero))
    inverse = 1.0 / jnp.sum(amount, axis=0, keepdims=True)
    delta = jnp.sum(weighted, axis=0, keepdims=True) * inverse

    def grads(j, acc):
        p = scores[j] * inverse
        g = p * (probs_grad[j] - delta)
        p = p.astype(BF16)
        g = g.astype(BF16)
        at = rows_of(j)
        dvalue[at, :] += dot_nn(p, douts)
        dkey[at, :] += dot_nn(g, queries)
        return acc + dot_nn(flipped[j], g)

    acc = lax.fori_loop(first, diag + 1, grads, jnp.zeros((width, chunk), F32))
    dq[...] = (acc.T * scale).astype(BF16)


def reduce_kernel(
    count, reach, heads, nblocks,
    doc, dec, parts, states, got_l1, got_l2, got_l3, got_r1, got_r2, got_r3, dkey, dvalue,
    dq, dk, dv, att_dk, att_dv,
    grads, near, echo, land, paired, out, inbox,
    pair_send, pair_recv, send_sem, recv_sem, echo_send, echo_recv,
):
    me = lax.axis_index("ctx")
    core = lax.axis_index("head")
    length = nblocks * TILE
    half = length // 2
    rows = TILE * heads
    width = dkey.shape[1]
    scale = dkey.shape[1] ** (-0.5)
    greet(me, core, count, reach)
    sources = (dkey, dvalue)

    def pair_copy(which, step):
        place = pl.multiple_of((reach - step) * length + (1 - core) * half, half)
        return pltpu.make_async_remote_copy(
            src_ref=sources[which].at[pl.ds(place, half)],
            dst_ref=paired.at[which, step],
            send_sem=pair_send.at[which, step],
            recv_sem=pair_recv.at[which, step],
            device_id={"head": 1 - core},
            device_id_type=MESH,
        )

    def home_copy(step):
        return pltpu.make_async_remote_copy(
            src_ref=out.at[step - 1],
            dst_ref=inbox.at[step - 1],
            send_sem=send_sem.at[step - 1],
            recv_sem=recv_sem.at[step - 1],
            device_id={"ctx": me - step},
            device_id_type=MESH,
        )

    order = list(range(reach, -1, -1))
    for step in order:
        pair_copy(0, step).start()
        pair_copy(1, step).start()

    follows, precedes, head_terms, t_sub, t_lane = decay_terms(me, count, nblocks, doc, dec)

    def echo_copy(side):
        return pltpu.make_async_remote_copy(
            src_ref=echo.at[side],
            dst_ref=land.at[side],
            send_sem=echo_send.at[side],
            recv_sem=echo_recv.at[side],
            device_id={"ctx": me + 3 if side == 0 else me - 3},
            device_id_type=MESH,
        )

    spans = ([], [])
    for side, got in enumerate(((got_l1, got_l2, got_l3), (got_r1, got_r2, got_r3))):
        for h in range(heads):
            mult = [
                ref[h, width : width + 16, :].astype(F32)[0:1]
                + ref[h, width + 16 : width + 32, :].astype(F32)[0:1]
                for ref in got
            ]
            one, two, three = (ref[h, 0:width, :].astype(F32) for ref in got)
            total = one + mult[0] * (two + mult[1] * three)
            near[side, h] = total
            echo[side, h] = total.astype(BF16)
            spans[side].append(mult[0] * mult[1] * mult[2])

    before = (me - 3 >= 0, me + 3 < count)
    after = (me + 3 < count, me - 3 >= 0)
    for side in range(2):

        @pl.when(after[side])
        def _():
            echo_copy(side).start()

        @pl.when(jnp.logical_not(before[side]))
        def _():
            land[side] = jnp.zeros(land.shape[1:], BF16)

    def within(b):
        for h in range(heads):
            row, col, total = head_terms(b, h)
            query, key, value, dout = (parts[a, b, h] for a in range(4))
            seen = t_sub <= t_lane
            weight = jnp.where(seen, jnp.exp(jnp.where(seen, row - col, 0.0)), 0.0)
            left = (dot_nt(value, dout) * weight).astype(BF16)
            right = (dot_nt(key, query) * weight).astype(BF16)
            at = pl.ds(b * rows + h, TILE, stride=heads)
            grads[0, at, :] = dot_tn(left, key)
            grads[1, at, :] = dot_nn(left, query)
            grads[2, at, :] = dot_nn(right, dout)

    within(0)

    def mine(which, step):
        place = pl.multiple_of((reach - step) * length + core * half, half)
        return sources[which][pl.ds(place, half), :] + paired[which, step]

    for step in order:
        for which in range(2):
            pair_copy(which, step).wait_recv()
        if step > 0:
            for which in range(2):
                out[step - 1, which] = mine(which, step).astype(BF16)

            @pl.when(me - step >= 0)
            def _():
                home_copy(step).start()

        if step > 0:

            @pl.when(me + step >= count)
            def _():
                inbox[step - 1] = jnp.zeros(inbox.shape[1:], BF16)

    for b in range(1, nblocks):
        within(b)
    for side in range(2):

        @pl.when(before[side])
        def _():
            echo_copy(side).wait_recv()

    for h in range(heads):
        keep = [jnp.exp(head_terms(b, h)[2]) for b in range(nblocks)]
        state = near[0, h] + spans[0][h] * land[0, h].astype(F32)
        into = []
        for b in range(nblocks):
            into.append(follows[b] * state)
            state = states[0, b, h] + keep[b] * into[b]
        state = near[1, h] + spans[1][h] * land[1, h].astype(F32)
        back = [None] * nblocks
        for b in reversed(range(nblocks)):
            back[b] = precedes[b] * state
            state = states[1, b, h] + keep[b] * back[b]
        for b in range(nblocks):
            row, col, total = head_terms(b, h)
            query, key, value, dout = (parts[a, b, h] for a in range(4))
            head_decay = jnp.exp(col)
            tail_decay = jnp.exp(total - col)
            into_high, into_low = split(into[b])
            back_high, back_low = split(back[b])
            at = pl.ds(b * rows + h, TILE, stride=heads)
            grads[0, at, :] = grads[0, at, :] + head_decay * (
                dot_nt(dout, into_high) + dot_nt(dout, into_low)
            )
            grads[1, at, :] = grads[1, at, :] + tail_decay * (
                dot_nt(value, back_high) + dot_nt(value, back_low)
            )
            grads[2, at, :] = grads[2, at, :] + tail_decay * (
                dot_nn(key, back_high) + dot_nn(key, back_low)
            )
    dq[...] = grads[0].astype(BF16)
    dk[...] = grads[1].astype(BF16)
    dv[...] = grads[2].astype(BF16)

    paired[0, 0] = mine(0, 0)
    paired[1, 0] = mine(1, 0)
    for step in range(1, reach + 1):

        @pl.when(me + step < count)
        def _():
            home_copy(step).wait_recv()

        for which in range(2):
            paired[which, 0] += inbox[step - 1, which].astype(F32)
    att_dk[...] = (paired[0, 0] * scale).astype(BF16)
    att_dv[...] = paired[1, 0].astype(BF16)
    for step in order:
        pair_copy(0, step).wait_send()
        pair_copy(1, step).wait_send()
        if step > 0:

            @pl.when(me - step >= 0)
            def _():
                home_copy(step).wait_send()
    for side in range(2):

        @pl.when(after[side])
        def _():
            echo_copy(side).wait_send()


def call_lightning(count, lin_q, lin_k, lin_v, lin_dout, lin_decay, att_k, att_v, doc_block):
    length, heads, width = lin_q.shape
    nblocks = length // TILE
    reach = -(-(MOST - 1) // nblocks)
    rows = length * heads
    window = (reach + 1) * length
    state = (heads, width, width)
    flat = lambda x: x.reshape(rows, width)
    return pl.pallas_call(
        functools.partial(lightning_kernel, count, reach, heads, nblocks),
        out_shape=[
            SHAPE((heads, width + 32, width), BF16),
            SHAPE((heads, width + 32, width), BF16),
            SHAPE((4, nblocks, heads, TILE, width), BF16),
            SHAPE((2, nblocks) + state, F32),
            SHAPE((window, width), BF16),
            SHAPE((window, width), BF16),
        ],
        in_specs=[IN_SMEM] + [ANYWHERE] * 7,
        out_specs=[IN_VMEM] * 4 + [ANYWHERE] * 2,
        scratch_shapes=[
            pltpu.VMEM((4, TILE * heads, width), F32),
            pltpu.VMEM((4, rows, width), BF16),
            pltpu.VMEM(lin_decay.shape, F32),
            DMA((5,)),
            DMA((2,)),
            DMA((2, reach)),
            DMA((2, reach)),
            DMA((2, reach)),
            DMA((2, reach)),
        ],
        compiler_params=pltpu.CompilerParams(
            collective_id=0, has_side_effects=True, vmem_limit_bytes=VMEM_LIMIT
        ),
        name="lightning",
    )(doc_block, flat(lin_q), flat(lin_k), flat(lin_v), flat(lin_dout), lin_decay, att_k, att_v)


def call_attention(chunk, spot, att_q, att_dout, kall, vall):
    length, heads, width = att_q.shape
    nblocks = length // TILE
    rows = length * heads
    window = kall.shape[0]
    reach = window // length - 1
    flat = lambda x: x.reshape(rows, width)
    return pl.pallas_call(
        functools.partial(attention_kernel, nblocks, reach, heads, chunk),
        grid_spec=pltpu.PrefetchScalarGridSpec(
            num_scalar_prefetch=1,
            grid=(rows // chunk,),
            in_specs=[
                pl.BlockSpec((chunk, width), lambda i, s: (i, 0)),
                pl.BlockSpec((chunk, width), lambda i, s: (i, 0)),
                pl.BlockSpec((window, width), lambda i, s: (0, 0)),
                pl.BlockSpec((window, width), lambda i, s: (0, 0)),
            ],
            out_specs=[
                pl.BlockSpec((chunk, width), lambda i, s: (i, 0)),
                pl.BlockSpec((window, width), lambda i, s: (0, 0)),
                pl.BlockSpec((window, width), lambda i, s: (0, 0)),
            ],
            scratch_shapes=[
                pltpu.VMEM((window // TILE, TILE, chunk), F32),
                pltpu.VMEM((window // TILE, TILE, chunk), F32),
                pltpu.VMEM((window // TILE, width, TILE), BF16),
            ],
        ),
        out_shape=[
            SHAPE((rows, width), BF16),
            SHAPE((window, width), F32),
            SHAPE((window, width), F32),
        ],
        compiler_params=pltpu.CompilerParams(vmem_limit_bytes=50 * 1024 * 1024),
        cost_estimate=pl.CostEstimate(
            flops=10 * width * rows * window, bytes_accessed=8 * window * width, transcendentals=0
        ),
        name="attention",
    )(spot, flat(att_q), flat(att_dout), kall, vall)


def shards(count, lin_q, lin_k, lin_v, lin_dout, lin_decay, att_q, att_k, att_v, att_dout, doc_block):
    length, heads, width = lin_q.shape
    nblocks = length // TILE
    reach = -(-(MOST - 1) // nblocks)
    half = length // 2
    rows = length * heads
    window = (reach + 1) * length
    send_l, send_r, parts, states, kall, vall = call_lightning(
        count, lin_q, lin_k, lin_v, lin_dout, lin_decay, att_k, att_v, doc_block
    )
    got = [
        lax.ppermute(send_l, "ctx", [(i, i + step) for i in range(count - step)])
        for step in (1, 2, 3)
    ] + [
        lax.ppermute(send_r, "ctx", [(i + step, i) for i in range(count - step)])
        for step in (1, 2, 3)
    ]
    me = lax.axis_index("ctx")
    here = lax.dynamic_slice_in_dim(doc_block, me * nblocks, nblocks)
    at = me * nblocks + jnp.arange(nblocks, dtype=jnp.int32)
    before = jnp.sum((doc_block[None, :] < here[:, None]).astype(jnp.int32), axis=1)
    spot = at - before + 1
    att_dq, dkey, dvalue = call_attention(1024, spot, att_q, att_dout, kall, vall)
    lin_dq, lin_dk, lin_dv, att_dk, att_dv = pl.pallas_call(
        functools.partial(reduce_kernel, count, reach, heads, nblocks),
        out_shape=[SHAPE((rows, width), BF16)] * 3 + [SHAPE((half, width), BF16)] * 2,
        in_specs=[IN_SMEM] + [IN_VMEM] * 11,
        out_specs=[IN_VMEM] * 5,
        scratch_shapes=[
            pltpu.VMEM((3, rows, width), F32),
            pltpu.VMEM((2, heads, width, width), F32),
            pltpu.VMEM((2, heads, width, width), BF16),
            pltpu.VMEM((2, heads, width, width), BF16),
            pltpu.VMEM((2, reach + 1, half, width), F32),
            pltpu.VMEM((reach, 2, half, width), BF16),
            pltpu.VMEM((reach, 2, half, width), BF16),
            DMA((2, reach + 1)),
            DMA((2, reach + 1)),
            DMA((reach,)),
            DMA((reach,)),
            DMA((2,)),
            DMA((2,)),
        ],
        compiler_params=pltpu.CompilerParams(
            collective_id=1, has_side_effects=True, vmem_limit_bytes=40 * 1024 * 1024
        ),
        name="reduce",
    )(doc_block, lin_decay, parts, states, *got, dkey, dvalue)
    full = lambda x: x.reshape(length, heads, width)
    return (full(lin_dq), full(lin_dk), full(lin_dv), full(att_dq), att_dk, att_dv)


def solution(mesh):
    return jax.shard_map(
        functools.partial(shards, mesh.shape["ctx"]),
        mesh=mesh,
        in_specs=(
            P("ctx", "head", None),
            P("ctx", "head", None),
            P("ctx", "head", None),
            P("ctx", "head", None),
            P("head", "ctx"),
            P("ctx", "head", None),
            P("ctx", None),
            P("ctx", None),
            P("ctx", "head", None),
            P(),
        ),
        out_specs=(
            P("ctx", "head", None),
            P("ctx", "head", None),
            P("ctx", "head", None),
            P("ctx", "head", None),
            P(("ctx", "head"), None),
            P(("ctx", "head"), None),
        ),
        check_vma=False,
    )
```
